256 devices in a mesh: dp: 2 (over x_lo), col: 32 (over y, z), row: 4 (over x_hi, core).
Axes of the slice: x: 4 (x_hi: 2, x_lo: 2; x = x_hi * 2 + x_lo), y: 4, z: 8, core: 2. Of those that a mesh axis runs over, the one named last changes fastest.
Arguments:
- cotangent: bfloat16 [4096, 7168], P(('dp', 'col'), 'row'), may hold values from -6 to 6
- codes: bfloat16 [7168, 20480], P('row', 'col'), may hold values from -1 to 1, as said below
- weight_scale: float32 [1], replicated, may hold values from 0.008 to 0.03
- rotated: bfloat16 [4096, 20480], P(('dp', 'row'), 'col'), may hold values from -6 to 6
- clip_level: float32 [4096], P(('dp', 'row')), may hold values from 0.5 to 3
Outputs:
- input_grad: bfloat16 [4096, 20480], P(('dp', 'row'), 'col')
- weight_grad: float32 [7168, 20480], P('row', 'col')
The draws below stay inside these ranges and needn't reach their ends.
Inputs may be any that keep to these rules, and one draw needn't show every extreme that they name: `codes`: every entry is -1, 0 or 1.
All inputs are finite; a program needn't handle non-finite values.
Results may differ from the reference program's by a relative error of at most 0.015.
Values may be sent and summed in bfloat16 or wider, within the bound.
No kernel may reach another device: no remote copies, remote signals or barrier semaphores. Data moves between devices by JAX's collectives and lax.ppermute only.
A program may use at most 64 MiB of HBM per device.

```python
import math
import jax
import jax.numpy as jnp
from jax import lax

D = 7168
FF = 20480
HB = 128
TOK_SHARD = 64
TOKENS = 4096
N_DP = 2
N_COL = 32
N_ROW = 4


def draw_codes(key, part):
    key = jax.random.fold_in(key, 11)
    values = jax.random.randint(key, (D, FF), -1, 2)
    return values.astype(jnp.float32).astype(jnp.bfloat16)


def levels(own_key, dims, shards, least, top_value):
    gain, own = 1.0, jax.random.fold_in(own_key, 6)
    for axis_at, parts in shards:
        heights = jnp.exp(jax.random.uniform(jax.random.fold_in(own, axis_at), (parts,), jnp.float32, least / len(shards), top_value / len(shards)))
        gain = gain * jnp.repeat(heights, dims[axis_at] // parts).reshape([-1 if axis == axis_at else 1 for axis in range(len(dims))])
    return gain


def scatter_about(own_key, extent, width, reach, cuts=(), kind=jnp.bfloat16):
    array = width * jax.random.normal(own_key, extent, jnp.float32)
    if cuts:
        array = array * levels(own_key, extent, cuts, -0.22, 0.18)
    return jnp.clip(array, -reach, reach).astype(kind)


def setup_inputs(seed: int = 0) -> dict:
    streams_of = jax.random.split(jax.random.key(seed), 6)
    return {
        "cotangent": scatter_about(streams_of[0], (TOKENS, D), 1.0, 6.0, ((0, 64), (1, 4))),
        "codes": draw_codes(jax.random.fold_in(streams_of[5], 71), 0),
        "weight_scale": jnp.clip(jnp.exp(jax.random.uniform(streams_of[2], (1,), jnp.float32, math.log(0.008), math.log(0.03))), 0.008, 0.03),
        "rotated": scatter_about(streams_of[3], (TOKENS, FF), 1.0, 6.0, ((0, 8), (1, 32))),
        "clip_level": jnp.clip(jnp.exp(math.log(3.0) - 1.7917595 * jax.random.uniform(streams_of[4], (TOKENS,), jnp.float32) ** levels(streams_of[4], (TOKENS,), ((0, 8),), -0.2, 0.2)), 0.5, 3.0),
    }


def hadamard_table(length):
    indices = jnp.arange(length, dtype=jnp.int32)
    parity = jnp.zeros((length, length), jnp.int32)
    for bit_place in range(length.bit_length() - 1):
        lower = indices[:, None] // 2 ** bit_place % 2
        upper = indices[None, :] // 2 ** bit_place % 2
        parity = parity + lower * upper
    signs = (1 - 2 * (parity % 2)).astype(jnp.float32)
    return signs / jnp.sqrt(jnp.float32(length))

def reference(cotangent, codes, weight_scale, rotated, clip_level):
    row_width = D // N_ROW
    group_rows = TOK_SHARD * N_COL
    act_grad = jnp.zeros((TOKENS, FF), jnp.float32)
    for row_index in range(N_ROW):
        partial_value = jnp.dot(cotangent[:, row_index * row_width:(row_index + 1) * row_width], codes[row_index * row_width:(row_index + 1) * row_width, :], preferred_element_type=jnp.float32) * weight_scale[0]
        partial_value = lax.optimization_barrier(partial_value.astype(jnp.bfloat16)).astype(jnp.float32)
        act_grad = act_grad + partial_value
    bound_col = clip_level[:, None]
    rotated_wide = rotated.astype(jnp.float32)
    masked = jnp.where(jnp.abs(rotated_wide) <= bound_col, act_grad, jnp.float32(0.0))
    rotation = hadamard_table(HB)
    blocks = masked.reshape(TOKENS, FF // HB, HB)
    input_grad = jnp.einsum('tbi,ij->tbj', blocks, rotation, precision=lax.Precision.HIGHEST).reshape(TOKENS, FF).astype(jnp.bfloat16)
    clipped = jnp.clip(rotated_wide, -bound_col, bound_col).astype(jnp.bfloat16)
    grad_norm = TOKENS ** (-0.5)
    weight_grad = jnp.zeros((D, FF), jnp.float32)
    for dp_index in range(N_DP):
        lower_row = dp_index * group_rows
        term = jnp.dot(cotangent[lower_row:lower_row + group_rows].T, clipped[lower_row:lower_row + group_rows], preferred_element_type=jnp.float32) * grad_norm
        term = lax.optimization_barrier(term.astype(jnp.bfloat16)).astype(jnp.float32)
        weight_grad = weight_grad + term
    return (input_grad, weight_grad)
```

```python
import functools

import jax
import jax.numpy as jnp
from jax import lax
from jax.experimental import pallas as pl
from jax.experimental.pallas import tpu as pltpu
from jax.sharding import PartitionSpec as P

HB = 128
NY, NZ = 4, 8
SHARD = 64
BF = jnp.bfloat16
F32 = jnp.float32

CHUNKS = (("zy", 1024), ("yz", 768))


def z_pairs(k):
    return [(y * NZ + z, y * NZ + (z + k) % NZ) for y in range(NY) for z in range(NZ)]


def y_pairs(k):
    return [(y * NZ + z, (y + k) % NY * NZ + z) for y in range(NY) for z in range(NZ)]


CORE = [(r, r ^ 1) for r in range(4)]
DP = [(0, 1), (1, 0)]
PARTNER = [(d * 4 + r, (1 - d) * 4 + (r ^ 2)) for d in range(2) for r in range(4)]
SWAP = [
    ((d * 32 + c) * 4 + r, ((d ^ (c // 16 != r // 2)) * 32 + c) * 4 + r)
    for d in range(2)
    for c in range(32)
    for r in range(4)
]


def gather_zy(shard):
    ups, downs = [shard], [shard]
    for _ in range(4):
        ups.append(lax.ppermute(ups[-1], "col", z_pairs(1)))
        if len(downs) < 4:
            downs.append(lax.ppermute(downs[-1], "col", z_pairs(-1)))
    line = jnp.concatenate(ups + downs[1:], axis=0)
    order = [0, -1, -2, -3, -4, 1, 2, 3]
    half = line.shape[0] // 2
    up = lax.ppermute(line, "col", y_pairs(1))
    down = lax.ppermute(line, "col", y_pairs(-1))
    up_far = lax.ppermute(up[:half], "col", y_pairs(1))
    down_far = lax.ppermute(down[half:], "col", y_pairs(-1))
    pieces = [line, up, down, up_far, down_far]
    places = [
        [(0, z) for z in order],
        [(-1, z) for z in order],
        [(1, z) for z in order],
        [(-2, z) for z in order[:4]],
        [(2, z) for z in order[4:]],
    ]
    return pieces, places


def gather_yz(shard):
    line = jnp.concatenate(
        [
            shard,
            lax.ppermute(shard, "col", y_pairs(1)),
            lax.ppermute(shard, "col", y_pairs(-1)),
            lax.ppermute(shard, "col", y_pairs(2)),
        ],
        axis=0,
    )
    order = [0, -1, 1, 2]
    half = line.shape[0] // 2
    pieces, places = [line], [[(y, 0) for y in order]]
    for sign in (1, -1):
        held = line
        for step in range(1, 4):
            held = lax.ppermute(held, "col", z_pairs(sign))
            pieces.append(held)
            places.append([(y, -sign * step) for y in order])
        if sign == 1:
            pieces.append(lax.ppermute(held[:half], "col", z_pairs(sign)))
            places.append([(y, 4) for y in order[:2]])
        else:
            pieces.append(lax.ppermute(held[half:], "col", z_pairs(sign)))
            places.append([(y, 4) for y in order[2:]])
    return pieces, places


def load_tokens(where, refs, places, held, sem):
    copies = []
    for ref, spots in zip(refs, places):
        for at, (dy, dz) in enumerate(spots):
            row = lax.rem(where[0] + dy + NY, NY) * NZ + lax.rem(where[1] + dz + NZ, NZ)
            copies.append(
                pltpu.make_async_copy(
                    ref.at[pl.ds(at * SHARD, SHARD)],
                    held.at[pl.ds(pl.multiple_of(row * SHARD, SHARD), SHARD)],
                    sem,
                )
            )
    return copies


def weight_kernel(places, scale, where, *refs):
    n = len(places)
    piece_refs, clip_refs, out, held, clip_held, sem = (
        refs[:n], refs[n:n + 4], refs[n + 4], refs[n + 5], refs[n + 6], refs[n + 7])
    copies = load_tokens(where, piece_refs, places, held, sem)
    rows = clip_refs[0].shape[0]
    for j, ref in enumerate(clip_refs):
        start = pl.multiple_of((where[2] ^ j) * rows, rows)
        copies.append(pltpu.make_async_copy(ref, clip_held.at[pl.ds(start, rows)], sem))
    for copy in copies:
        copy.start()
    for copy in copies:
        copy.wait()
    width = out.shape[0]
    for lo in range(0, width, 256):
        size = min(256, width - lo)
        out[lo:lo + size, :] = (
            lax.dot_general(
                held[:, lo:lo + size], clip_held[...], (((0,), (0,)), ((), ())),
                preferred_element_type=F32,
            ) * scale
        ).astype(BF)


def weight_term(where, pieces, places, clips, scale):
    width = pieces[0].shape[1]
    tokens = 4 * clips[0].shape[0]
    cols = clips[0].shape[1]
    anywhere = pl.BlockSpec(memory_space=pl.ANY)
    return pl.pallas_call(
        functools.partial(weight_kernel, places, scale),
        out_shape=jax.ShapeDtypeStruct((width, cols), BF),
        in_specs=[pl.BlockSpec(memory_space=pltpu.SMEM)] + [anywhere] * (len(pieces) + 4),
        out_specs=pl.BlockSpec(memory_space=pltpu.VMEM),
        scratch_shapes=[
            pltpu.VMEM((tokens, width), BF),
            pltpu.VMEM((tokens, cols), BF),
            pltpu.SemaphoreType.DMA,
        ],
        compiler_params=pltpu.CompilerParams(vmem_limit_bytes=48 * 2**20),
        cost_estimate=pl.CostEstimate(
            flops=2 * tokens * width * cols,
            bytes_accessed=2 * (tokens * (width + cols) + width * cols),
            transcendentals=0),
        name="weight_term",
    )(where, *pieces, *clips)


def act_kernel(all_places, starts, where, weight_scale, codes, *refs):
    n = sum(len(p) for p in all_places)
    piece_refs = refs[:n]
    outs, held, code_held, sem = refs[n:n + 4], refs[n + 4], refs[n + 5], refs[n + 6]
    copies = [pltpu.make_async_copy(codes, code_held, sem)]
    at = 0
    for places, start in zip(all_places, starts):
        here = piece_refs[at:at + len(places)]
        at += len(places)
        width = here[0].shape[1]
        copies += load_tokens(where, here, places, held.at[:, pl.ds(start, width)], sem)
    for copy in copies:
        copy.start()
    for copy in copies:
        copy.wait()
    rows = outs[0].shape[0]
    for j in (3, 2, 1, 0):
        start = pl.multiple_of((where[2] ^ j) * rows, rows)
        outs[j][...] = (
            jnp.dot(held[pl.ds(start, rows), :], code_held[...], preferred_element_type=F32)
            * weight_scale[0]
        ).astype(BF)


def act_parts(where, weight_scale, codes, gathered, starts):
    depth, cols = codes.shape
    tokens = 2048
    pieces = [p for g in gathered for p in g[0]]
    anywhere = pl.BlockSpec(memory_space=pl.ANY)
    smem = pl.BlockSpec(memory_space=pltpu.SMEM)
    return pl.pallas_call(
        functools.partial(act_kernel, [g[1] for g in gathered], starts),
        out_shape=[jax.ShapeDtypeStruct((tokens // 4, cols), BF)] * 4,
        in_specs=[smem, smem] + [anywhere] * (len(pieces) + 1),
        out_specs=[pl.BlockSpec(memory_space=pltpu.VMEM)] * 4,
        scratch_shapes=[
            pltpu.VMEM((tokens, depth), BF),
            pltpu.VMEM((depth, cols), BF),
            pltpu.SemaphoreType.DMA,
        ],
        compiler_params=pltpu.CompilerParams(vmem_limit_bytes=48 * 2**20),
        cost_estimate=pl.CostEstimate(
            flops=2 * tokens * depth * cols,
            bytes_accessed=2 * (tokens * (depth + cols) + depth * cols),
            transcendentals=0),
        name="act_parts",
    )(where, weight_scale, codes, *pieces)


def finish_kernel(own, sibling, other, rotated, bound, signs, out):
    summed = own[...].astype(F32) + sibling[...].astype(F32) + other[...].astype(F32)
    masked = jnp.where(jnp.abs(rotated[...].astype(F32)) <= bound[...], summed, 0.0)
    high = masked.astype(BF)
    low = (masked - high.astype(F32)).astype(BF)
    table = signs[...]
    for lo in range(0, out.shape[1], HB):
        turned = jnp.dot(high[:, lo:lo + HB], table, preferred_element_type=F32)
        turned += jnp.dot(low[:, lo:lo + HB], table, preferred_element_type=F32)
        out[:, lo:lo + HB] = (turned * (HB ** -0.5)).astype(BF)


def finish(own, sibling, other, rotated, bound, signs):
    vmem = pl.BlockSpec(memory_space=pltpu.VMEM)
    return pl.pallas_call(
        finish_kernel,
        out_shape=jax.ShapeDtypeStruct(own.shape, BF),
        in_specs=[vmem] * 6,
        out_specs=vmem,
        compiler_params=pltpu.CompilerParams(vmem_limit_bytes=48 * 2**20),
        name="finish",
    )(own, sibling, other, rotated, bound, signs)


def hadamard_signs(length):
    indices = jnp.arange(length, dtype=jnp.int32)
    common = indices[:, None] & indices[None, :]
    parity = jnp.zeros((length, length), jnp.int32)
    for bit in range(length.bit_length() - 1):
        parity = parity ^ (common >> bit)
    return (1 - 2 * (parity & 1)).astype(BF)


def body(cotangent, codes, weight_scale, rotated, clip_level):
    col = lax.axis_index("col")
    row = lax.axis_index("row")
    where = jnp.stack([col // NZ, col % NZ, row]).astype(jnp.int32)
    token_total = cotangent.shape[0] * lax.axis_size("col") * lax.axis_size("dp")
    grad_norm = token_total ** (-0.5)

    gathered, starts, lo = [], [], 0
    for kind, width in CHUNKS:
        shard = lax.ppermute(cotangent[:, lo:lo + width], ("dp", "col", "row"), SWAP)
        gathered.append((gather_zy if kind == "zy" else gather_yz)(shard))
        starts.append(lo)
        lo += width

    bound = clip_level[:, None]
    clipped = jnp.clip(rotated.astype(F32), -bound, bound).astype(BF)
    other = lax.ppermute(clipped, ("dp", "row"), PARTNER)
    clips = [
        clipped,
        lax.ppermute(clipped, "row", CORE),
        other,
        lax.ppermute(other, "row", CORE),
    ]

    terms = []
    for pieces, places in gathered:
        mine = weight_term(where, pieces, places, clips, grad_norm)
        theirs = lax.ppermute(mine, "dp", DP)
        terms.append(mine.astype(F32) + theirs.astype(F32))
    weight_grad = jnp.concatenate(terms, axis=0)

    parts = act_parts(where, weight_scale, codes, gathered, starts)
    from_sibling = lax.ppermute(parts[3], "row", CORE)
    outward = (parts[2].astype(F32) + from_sibling.astype(F32)).astype(BF)
    inward = lax.ppermute(outward, ("dp", "row"), PARTNER)
    sibling = lax.ppermute(parts[1], "row", CORE)
    input_grad = finish(parts[0], sibling, inward, rotated, bound, hadamard_signs(HB))
    return (input_grad, weight_grad)


def solution(mesh):
    placed = (
        P(("dp", "col"), "row"),
        P("row", "col"),
        P(),
        P(("dp", "row"), "col"),
        P(("dp", "row")),
    )
    return jax.shard_map(
        body,
        mesh=mesh,
        in_specs=placed,
        out_specs=(P(("dp", "row"), "col"), P("row", "col")),
        check_vma=False,
    )
```

```python
import functools

import jax
import jax.numpy as jnp
from jax import lax
from jax.experimental import pallas as pl
from jax.experimental.pallas import tpu as pltpu
from jax.sharding import PartitionSpec as P

HB = 128
NY, NZ = 4, 8
SHARD = 64
BF = jnp.bfloat16
F32 = jnp.float32

WIDTHS = (1024, 768)
VMEM = 60 * 2**20
SMALL = 16 * 2**20
HALF = 512
LITTLE = pl.CostEstimate(flops=1, bytes_accessed=1, transcendentals=0)

NEAR = (-2, -1, 0, 1)
FAR = (-4, -3, 2, 3)
Y_ORDER = (0, -1, 1, -2)
PIECES = 10


def z_pairs(k):
    return [(y * NZ + z, y * NZ + (z + k) % NZ) for y in range(NY) for z in range(NZ)]


def y_pairs(k):
    return [(y * NZ + z, (y + k) % NY * NZ + z) for y in range(NY) for z in range(NZ)]


CORE = [(r, r ^ 1) for r in range(4)]
DP = [(0, 1), (1, 0)]
PARTNER = [(d * 4 + r, (1 - d) * 4 + (r ^ 2)) for d in range(2) for r in range(4)]


def pairs_for(steps, swap=False):
    pairs = []
    for d in range(2):
        for y in range(NY):
            for z in range(NZ):
                for r in range(4):
                    step = steps[r % 2]
                    if step is None:
                        continue
                    there = d ^ (y // 2 != r // 2) if swap else d
                    target = (y + step[0]) % NY * NZ + (z + step[1]) % NZ
                    pairs.append((((d * 32) + y * NZ + z) * 4 + r, (there * 32 + target) * 4 + r))
    return pairs


def move(value, core0, core1, swap=False):
    return lax.ppermute(value, ("dp", "col", "row"), pairs_for((core0, core1), swap))


def join_kernel(*refs):
    for at, shard in enumerate(refs[:4]):
        lo = 0
        for out in refs[4:]:
            width = out.shape[1]
            out[at * SHARD:(at + 1) * SHARD, :] = shard[:, lo:lo + width]
            lo += width


def join(*shards):
    vmem = pl.BlockSpec(memory_space=pltpu.VMEM)
    return list(pl.pallas_call(
        join_kernel,
        out_shape=[jax.ShapeDtypeStruct((4 * SHARD, width), BF) for width in WIDTHS],
        in_specs=[vmem] * 4,
        out_specs=[vmem] * len(WIDTHS),
        compiler_params=pltpu.CompilerParams(vmem_limit_bytes=SMALL),
        cost_estimate=LITTLE,
        name="join",
    )(*shards))


def gather(own, first_core, before_second, before_third):
    a = move(own, (0, 1), (1, 0))
    b = move(own, (0, -1), (-1, 0))
    c = move(own, (0, 2), (2, 0))
    near = join(c, a, own, b)
    up1 = [move(part, (1, 0), (0, 1)) for part in near]
    down1 = [move(part, (-1, 0), (0, -1)) for part in near]
    far_up = move(c, (0, 1), None)
    far_down = move(b, (0, -1), None)
    up1[0], down1[0], far_up, far_down = before_second(up1[0], down1[0], far_up, far_down)
    up2 = [move(part, (1, 0), (0, 1)) for part in up1]
    down2 = [move(part, None, (0, -1)) for part in down1]
    far = join(move(far_up, (0, 1), None), far_up, far_down, move(far_down, (0, -1), None))
    up2[0], down2[0], up1[1], down1[1] = before_third(up2[0], down2[0], up1[1], down1[1])
    up3 = [move(jnp.where(first_core, f, part), (1, 0), (0, 1)) for f, part in zip(far, up2)]
    down3 = [move(jnp.where(first_core, f, part), (-1, 0), (0, -1)) for f, part in zip(far, down2)]
    up3[0], down3[0], up2[1], down2[1] = lax.optimization_barrier((up3[0], down3[0], up2[1], down2[1]))
    up4 = [move(part[:2 * SHARD], (1, 0), (0, 1)) for part in up3]
    down4 = [move(part[2 * SHARD:], (-1, 0), (0, -1)) for part in down3]
    return [list(group) for group in zip(near, far, up1, down1, up2, down2, up3, down3, up4, down4)]


def places_of(core):
    if core == 0:
        lines = ((0, NEAR), (0, FAR), (-1, NEAR), (1, NEAR), (-2, NEAR), (0, ()), (-1, FAR), (1, FAR),
                 (-2, FAR[:2]), (-2, FAR[2:]))
        return [[(dy, dz) for dz in line] for dy, line in lines]
    lines = ((0, NEAR), (0, ()), (-1, NEAR), (1, NEAR), (-2, NEAR), (2, NEAR), (-3, NEAR), (3, NEAR),
             (-4, NEAR[:2]), (4, NEAR[2:]))
    return [[(dy, dz) for dy in line] for dz, line in lines]


def each_shard(where, refs, do, turns=Y_ORDER):
    for core in range(2):
        @pl.when(where[2] % 2 == core)
        def _():
            for turn in turns:
                for ref, spots in zip(refs, places_of(core)):
                    for at, (dy, dz) in enumerate(spots):
                        if dy == turn:
                            do(ref.at[pl.ds(at * SHARD, SHARD)],
                               lax.rem(where[0] + dy + NY, NY), lax.rem(where[1] + dz + NZ, NZ))


def clip_kernel(rotated, bound, out):
    top = bound[...]
    for lo in range(0, rotated.shape[1], 128):
        block = jnp.clip(rotated[:, lo:lo + 128].astype(F32), -top, top)
        out[lo:lo + 128, :] = block.T.astype(BF)


def clip_turned(rotated, bound):
    vmem = pl.BlockSpec(memory_space=pltpu.VMEM)
    return pl.pallas_call(
        clip_kernel,
        out_shape=jax.ShapeDtypeStruct(rotated.shape[::-1], BF),
        in_specs=[vmem] * 2,
        out_specs=vmem,
        compiler_params=pltpu.CompilerParams(vmem_limit_bytes=SMALL),
        name="clip_turned",
    )(rotated, bound)


def weight_kernel(scale, where, *refs):
    n = PIECES
    piece_refs, (own, both, other) = refs[:n], refs[n:n + 3]
    out, held, clip_held, sem, clip_sem = refs[n + 3:]
    cols, size = own.shape
    for j, ref in enumerate((own, both.at[pl.ds(0, cols)], other, both.at[pl.ds(cols, cols)])):
        start = pl.multiple_of((where[2] ^ j) * size, size)
        pltpu.make_async_copy(ref, clip_held.at[:, pl.ds(start, size)], clip_sem).start()
    width = out.shape[1]
    windows = ((0, HALF), (HALF, width))
    for i, (lo, hi) in enumerate(windows):
        window = pl.ds(lo, hi - lo)

        def load(ref, y, z):
            spot = pl.ds(pl.multiple_of((y * NZ + z) * SHARD, SHARD), SHARD)
            pltpu.make_async_copy(ref.at[:, window], held.at[spot, window], sem.at[i]).start()

        each_shard(where, piece_refs, load)
    pltpu.make_async_copy(clip_held, clip_held, clip_sem).wait()
    for i, (lo, hi) in enumerate(windows):
        part = held.at[:, pl.ds(lo, hi - lo)]
        pltpu.make_async_copy(part, part, sem.at[i]).wait()
        for first in range(lo, hi, 256):
            step = min(256, hi - first)
            out[:, first:first + step] = (
                jnp.dot(clip_held[...], held[:, first:first + step], preferred_element_type=F32) * scale
            ).astype(BF)


def weight_term(where, pieces, clips, scale):
    width = pieces[0].shape[1]
    cols, part = clips[0].shape
    tokens = 4 * part
    anywhere = pl.BlockSpec(memory_space=pltpu.HBM)
    return pl.pallas_call(
        functools.partial(weight_kernel, scale),
        out_shape=jax.ShapeDtypeStruct((cols, width), BF),
        in_specs=[pl.BlockSpec(memory_space=pltpu.SMEM)] + [anywhere] * (len(pieces) + 3),
        out_specs=pl.BlockSpec(memory_space=pltpu.VMEM),
        scratch_shapes=[
            pltpu.VMEM((tokens, width), BF),
            pltpu.VMEM((cols, tokens), BF),
            pltpu.SemaphoreType.DMA((2,)),
            pltpu.SemaphoreType.DMA,
        ],
        compiler_params=pltpu.CompilerParams(vmem_limit_bytes=VMEM),
        cost_estimate=LITTLE,
        name="weight_term",
    )(where, *pieces, *clips)


def sum_kernel(lo, mine, theirs, *refs):
    out, held, sem = refs[-3:]
    width = mine.shape[1]
    copies = []
    for at in range(0, width, 128):
        both = mine[:, at:at + 128].astype(F32) + theirs[:, at:at + 128].astype(F32)
        held[at:at + 128, :] = both.T
        copies.append(pltpu.make_async_copy(
            held.at[pl.ds(at, 128)], out.at[pl.ds(lo + at, 128)], sem.at[at // 128]))
        copies[-1].start()
    for copy in copies:
        copy.wait()


def sum_terms(lo, mine, theirs, whole, depth):
    cols, width = mine.shape
    vmem = pl.BlockSpec(memory_space=pltpu.VMEM)
    anywhere = pl.BlockSpec(memory_space=pltpu.HBM)
    before = [] if whole is None else [whole]
    return pl.pallas_call(
        functools.partial(sum_kernel, lo),
        out_shape=jax.ShapeDtypeStruct((depth, cols), F32),
        in_specs=[vmem] * 2 + [anywhere] * len(before),
        out_specs=anywhere,
        scratch_shapes=[pltpu.VMEM((width, cols), F32), pltpu.SemaphoreType.DMA((width // 128,))],
        input_output_aliases={2: 0} if before else {},
        compiler_params=pltpu.CompilerParams(vmem_limit_bytes=SMALL),
        name="sum_terms",
    )(mine, theirs, *before)


def act_kernel(where, weight_scale, codes, *refs):
    n = PIECES * len(WIDTHS)
    piece_refs, (out, held, code_held, sem, code_sem) = refs[:n], refs[n:]
    code_copy = pltpu.make_async_copy(codes, code_held, code_sem)
    code_copy.start()
    rows = held.shape[1]
    for turn in Y_ORDER:
        lo = 0
        for i, width in enumerate(WIDTHS):
            window = pl.ds(lo, width)
            lo += width

            def load(ref, y, z):
                spot = pl.ds(pl.multiple_of(z * SHARD, SHARD), SHARD)
                pltpu.make_async_copy(ref, held.at[y, spot, window], sem.at[y]).start()

            each_shard(where, piece_refs[i * PIECES:(i + 1) * PIECES], load, (turn,))
    code_copy.wait()
    for turn in Y_ORDER:
        y = lax.rem(where[0] + turn + NY, NY)
        pltpu.make_async_copy(held.at[y], held.at[y], sem.at[y]).wait()
        total = jnp.dot(held[y], code_held[...], preferred_element_type=F32) * weight_scale[0]
        j = y ^ where[2]
        place = 2 * (1 - j % 2) + 1 - j // 2
        out[pl.ds(pl.multiple_of(place * rows, rows), rows), :] = total.astype(BF)


def act_parts(where, weight_scale, codes, groups):
    depth, cols = codes.shape
    rows = 8 * SHARD
    pieces = [piece for group in groups for piece in group]
    anywhere = pl.BlockSpec(memory_space=pltpu.HBM)
    smem = pl.BlockSpec(memory_space=pltpu.SMEM)
    return pl.pallas_call(
        act_kernel,
        out_shape=jax.ShapeDtypeStruct((4 * rows, cols), BF),
        in_specs=[smem, smem] + [anywhere] * (len(pieces) + 1),
        out_specs=pl.BlockSpec(memory_space=pltpu.VMEM),
        scratch_shapes=[
            pltpu.VMEM((4, rows, depth), BF),
            pltpu.VMEM((depth, cols), BF),
            pltpu.SemaphoreType.DMA((4,)),
            pltpu.SemaphoreType.DMA,
        ],
        compiler_params=pltpu.CompilerParams(vmem_limit_bytes=VMEM),
        cost_estimate=LITTLE,
        name="act_parts",
    )(where, weight_scale, codes, *pieces)


def finish_kernel(parts, got, other, rotated, bound, signs, out):
    rows = out.shape[0]
    summed = parts[3 * rows:, :].astype(F32) + got[rows:, :].astype(F32) + other[...].astype(F32)
    masked = jnp.where(jnp.abs(rotated[...].astype(F32)) <= bound[...], summed, 0.0)
    high = masked.astype(BF)
    low = (masked - high.astype(F32)).astype(BF)
    table = signs[...]
    for lo in range(0, out.shape[1], HB):
        turned = jnp.dot(high[:, lo:lo + HB], table, preferred_element_type=F32)
        turned += jnp.dot(low[:, lo:lo + HB], table, preferred_element_type=F32)
        out[:, lo:lo + HB] = (turned * (HB ** -0.5)).astype(BF)


def finish(parts, got, other, rotated, bound, signs):
    vmem = pl.BlockSpec(memory_space=pltpu.VMEM)
    return pl.pallas_call(
        finish_kernel,
        out_shape=jax.ShapeDtypeStruct(other.shape, BF),
        in_specs=[vmem] * 6,
        out_specs=vmem,
        compiler_params=pltpu.CompilerParams(vmem_limit_bytes=SMALL),
        name="finish",
    )(parts, got, other, rotated, bound, signs)


def hadamard_signs(length):
    indices = jnp.arange(length, dtype=jnp.int32)
    common = indices[:, None] & indices[None, :]
    parity = jnp.zeros((length, length), jnp.int32)
    for bit in range(length.bit_length() - 1):
        parity = parity ^ (common >> bit)
    return (1 - 2 * (parity & 1)).astype(BF)


def body(cotangent, codes, weight_scale, rotated, clip_level):
    col = lax.axis_index("col")
    row = lax.axis_index("row")
    where = jnp.stack([col // NZ, col % NZ, row]).astype(jnp.int32)
    token_total = cotangent.shape[0] * lax.axis_size("col") * lax.axis_size("dp")
    grad_norm = token_total ** (-0.5)

    bound = clip_level[:, None]
    clipped = clip_turned(rotated, bound)
    other = lax.ppermute(clipped, ("dp", "row"), PARTNER)

    tie = lax.optimization_barrier
    first_core = row % 2 == 0
    both = None

    def before_second(*arrays):
        nonlocal other, both
        *arrays, other = tie((*arrays, other))
        both = lax.ppermute(jnp.concatenate([clipped, other], axis=0), "row", CORE)
        return arrays

    def before_third(*arrays):
        nonlocal both
        *arrays, both = tie((*arrays, both))
        return arrays

    own = move(cotangent, (0, 0), (0, 0), True)
    groups = gather(own, first_core, before_second, before_third)
    clips = [clipped, both, other]
    mine0 = weight_term(where, groups[0], clips, grad_norm)
    theirs0 = lax.ppermute(mine0, "dp", DP)
    mine0, groups[0][0] = tie((mine0, groups[0][0]))
    rows = clipped.shape[1]
    parts = act_parts(where, weight_scale, codes, groups)
    parts, groups[1][0] = tie((parts, groups[1][0]))
    mine1 = weight_term(where, groups[1], clips, grad_norm)
    got = lax.ppermute(parts[:2 * rows], "row", CORE)
    mine1, theirs0 = tie((mine1, theirs0))
    theirs1 = lax.ppermute(mine1, "dp", DP)
    outward = (parts[2 * rows:3 * rows].astype(F32) + got[:rows].astype(F32)).astype(BF)
    inward = lax.ppermute(outward, ("dp", "row"), PARTNER)
    weight_grad = sum_terms(0, mine0, theirs0, None, codes.shape[0])
    input_grad = finish(parts, got, inward, rotated, bound, hadamard_signs(HB))
    input_grad, theirs1 = tie((input_grad, theirs1))
    weight_grad = sum_terms(WIDTHS[0], mine1, theirs1, weight_grad, codes.shape[0])
    return (input_grad, weight_grad)


def solution(mesh):
    placed = (
        P(("dp", "col"), "row"),
        P("row", "col"),
        P(),
        P(("dp", "row"), "col"),
        P(("dp", "row")),
    )
    return jax.shard_map(
        body,
        mesh=mesh,
        in_specs=placed,
        out_specs=(P(("dp", "row"), "col"), P("row", "col")),
        check_vma=False,
    )
```

```python
import functools

import jax
import jax.numpy as jnp
from jax import lax
from jax.experimental import pallas as pl
from jax.experimental.pallas import tpu as pltpu
from jax.sharding import PartitionSpec as P

HB = 128
NY, NZ = 4, 8
SHARD = 64
BF = jnp.bfloat16
F32 = jnp.float32

WIDTHS = (896, 896)
VMEM = 60 * 2**20
SMALL = 16 * 2**20
HALF = 512
LITTLE = pl.CostEstimate(flops=1, bytes_accessed=1, transcendentals=0)

NEAR = (-2, -1, 0, 1)
FAR = (-4, -3, 2, 3)
Y_ORDER = (0, -1, 1, -2)
PIECES = 10


def z_pairs(k):
    return [(y * NZ + z, y * NZ + (z + k) % NZ) for y in range(NY) for z in range(NZ)]


def y_pairs(k):
    return [(y * NZ + z, (y + k) % NY * NZ + z) for y in range(NY) for z in range(NZ)]


CORE = [(r, r ^ 1) for r in range(4)]
DP = [(0, 1), (1, 0)]
PARTNER_SIBLING = [(d * 4 + r, (1 - d) * 4 + (r ^ 3)) for d in range(2) for r in range(4)]
PARTNER = [(d * 4 + r, (1 - d) * 4 + (r ^ 2)) for d in range(2) for r in range(4)]


def pairs_for(steps, swap=False):
    pairs = []
    for d in range(2):
        for y in range(NY):
            for z in range(NZ):
                for r in range(4):
                    step = steps[r % 2]
                    if step is None:
                        continue
                    there = d ^ (y // 2 != r // 2) if swap else d
                    target = (y + step[0]) % NY * NZ + (z + step[1]) % NZ
                    pairs.append((((d * 32) + y * NZ + z) * 4 + r, (there * 32 + target) * 4 + r))
    return pairs


def move(value, core0, core1, swap=False):
    return lax.ppermute(value, ("dp", "col", "row"), pairs_for((core0, core1), swap))


def near_kernel(c, a, own, b, *outs):
    for i, shard in enumerate((c, a, own, b)):
        lo = 0
        for out in outs[:-2]:
            width = out.shape[1]
            out[i * SHARD:(i + 1) * SHARD, :] = shard[:, lo:lo + width]
            lo += width
        outs[-2 + i // 2][i % 2 * SHARD:(i % 2 + 1) * SHARD, :] = shard[...]


def far_kernel(low, high, *outs):
    lo = 0
    for out in outs:
        width = out.shape[1]
        out[:2 * SHARD, :] = low[:, lo:lo + width]
        out[2 * SHARD:, :] = high[:, lo:lo + width]
        lo += width


def join(kernel, shards, extra):
    vmem = pl.BlockSpec(memory_space=pltpu.VMEM)
    shapes = [(4 * SHARD, width) for width in WIDTHS] + extra
    return list(pl.pallas_call(
        kernel,
        out_shape=[jax.ShapeDtypeStruct(shape, BF) for shape in shapes],
        in_specs=[vmem] * len(shards),
        out_specs=[vmem] * len(shapes),
        compiler_params=pltpu.CompilerParams(vmem_limit_bytes=SMALL),
        cost_estimate=LITTLE,
        name="join",
    )(*shards))


def gather(own, first_core, before_second):
    a = move(own, (0, 1), (1, 0))
    b = move(own, (0, -1), (-1, 0))
    c = move(own, (0, 2), (2, 0))
    *near, low, high = join(near_kernel, (c, a, own, b), [(2 * SHARD, own.shape[1])] * 2)
    up1 = [move(near[0], (1, 0), (0, 1))]
    down1 = [move(near[0], (-1, 0), (0, -1))]
    low = move(low, (0, 2), None)
    high = move(high, (0, -2), None)
    near[1], low, high = before_second(near[1], low, high)
    up1.append(move(near[1], (1, 0), (0, 1)))
    down1.append(move(near[1], (-1, 0), (0, -1)))
    up2 = [move(part, (1, 0), (0, 1)) for part in up1]
    down2 = [move(part, None, (0, -1)) for part in down1]
    far = join(far_kernel, (low, high), [])
    up3 = [move(jnp.where(first_core, f, part), (1, 0), (0, 1)) for f, part in zip(far, up2)]
    down3 = [move(jnp.where(first_core, f, part), (-1, 0), (0, -1)) for f, part in zip(far, down2)]
    up4 = [move(part[:2 * SHARD], (1, 0), (0, 1)) for part in up3]
    down4 = [move(part[2 * SHARD:], (-1, 0), (0, -1)) for part in down3]
    return [list(group) for group in zip(near, far, up1, down1, up2, down2, up3, down3, up4, down4)]


def places_of(core):
    if core == 0:
        lines = ((0, NEAR), (0, FAR), (-1, NEAR), (1, NEAR), (-2, NEAR), (0, ()), (-1, FAR), (1, FAR),
                 (-2, FAR[:2]), (-2, FAR[2:]))
        return [[(dy, dz) for dz in line] for dy, line in lines]
    lines = ((0, NEAR), (0, ()), (-1, NEAR), (1, NEAR), (-2, NEAR), (2, NEAR), (-3, NEAR), (3, NEAR),
             (-4, NEAR[:2]), (4, NEAR[2:]))
    return [[(dy, dz) for dy in line] for dz, line in lines]


def each_shard(where, refs, do, turns=Y_ORDER):
    for core in range(2):
        @pl.when(where[2] % 2 == core)
        def _():
            for turn in turns:
                for ref, spots in zip(refs, places_of(core)):
                    for at, (dy, dz) in enumerate(spots):
                        if dy == turn:
                            do(ref.at[pl.ds(at * SHARD, SHARD)],
                               lax.rem(where[0] + dy + NY, NY), lax.rem(where[1] + dz + NZ, NZ))


def clip_kernel(rotated, bound, out):
    top = bound[...]
    for lo in range(0, rotated.shape[1], 128):
        block = jnp.clip(rotated[:, lo:lo + 128].astype(F32), -top, top)
        out[lo:lo + 128, :] = block.T.astype(BF)


def clip_turned(rotated, bound):
    vmem = pl.BlockSpec(memory_space=pltpu.VMEM)
    return pl.pallas_call(
        clip_kernel,
        out_shape=jax.ShapeDtypeStruct(rotated.shape[::-1], BF),
        in_specs=[vmem] * 2,
        out_specs=vmem,
        compiler_params=pltpu.CompilerParams(vmem_limit_bytes=SMALL),
        name="clip_turned",
    )(rotated, bound)


def weight_kernel(scale, where, *refs):
    n = PIECES
    piece_refs, clip_refs = refs[:n], refs[n:n + 4]
    out, held, clip_held, sem, clip_sem = refs[n + 4:]
    for j, ref in enumerate(clip_refs):
        size = ref.shape[1]
        start = pl.multiple_of((where[2] ^ j) * size, size)
        pltpu.make_async_copy(ref, clip_held.at[:, pl.ds(start, size)], clip_sem).start()
    width = out.shape[1]
    windows = ((0, HALF), (HALF, width))
    for i, (lo, hi) in enumerate(windows):
        window = pl.ds(lo, hi - lo)

        def load(ref, y, z):
            spot = pl.ds(pl.multiple_of((y * NZ + z) * SHARD, SHARD), SHARD)
            pltpu.make_async_copy(ref.at[:, window], held.at[spot, window], sem.at[i]).start()

        each_shard(where, piece_refs, load)
    pltpu.make_async_copy(clip_held, clip_held, clip_sem).wait()
    for i, (lo, hi) in enumerate(windows):
        part = held.at[:, pl.ds(lo, hi - lo)]
        pltpu.make_async_copy(part, part, sem.at[i]).wait()
        for first in range(lo, hi, 256):
            step = min(256, hi - first)
            out[:, first:first + step] = (
                jnp.dot(clip_held[...], held[:, first:first + step], preferred_element_type=F32) * scale
            ).astype(BF)


def weight_term(where, pieces, clips, scale):
    width = pieces[0].shape[1]
    cols, part = clips[0].shape
    tokens = 4 * part
    anywhere = pl.BlockSpec(memory_space=pltpu.HBM)
    return pl.pallas_call(
        functools.partial(weight_kernel, scale),
        out_shape=jax.ShapeDtypeStruct((cols, width), BF),
        in_specs=[pl.BlockSpec(memory_space=pltpu.SMEM)] + [anywhere] * (len(pieces) + 4),
        out_specs=pl.BlockSpec(memory_space=pltpu.VMEM),
        scratch_shapes=[
            pltpu.VMEM((tokens, width), BF),
            pltpu.VMEM((cols, tokens), BF),
            pltpu.SemaphoreType.DMA((2,)),
            pltpu.SemaphoreType.DMA,
        ],
        compiler_params=pltpu.CompilerParams(vmem_limit_bytes=VMEM),
        cost_estimate=LITTLE,
        name="weight_term",
    )(where, *pieces, *clips)


def sum_kernel(lo, mine, theirs, *refs):
    out, held, sem = refs[-3:]
    width = mine.shape[1]
    copies = []
    for at in range(0, width, 128):
        both = mine[:, at:at + 128].astype(F32) + theirs[:, at:at + 128].astype(F32)
        held[at:at + 128, :] = both.T
        copies.append(pltpu.make_async_copy(
            held.at[pl.ds(at, 128)], out.at[pl.ds(lo + at, 128)], sem.at[at // 128]))
        copies[-1].start()
    for copy in copies:
        copy.wait()


def sum_terms(lo, mine, theirs, whole, depth):
    cols, width = mine.shape
    vmem = pl.BlockSpec(memory_space=pltpu.VMEM)
    anywhere = pl.BlockSpec(memory_space=pltpu.HBM)
    before = [] if whole is None else [whole]
    return pl.pallas_call(
        functools.partial(sum_kernel, lo),
        out_shape=jax.ShapeDtypeStruct((depth, cols), F32),
        in_specs=[vmem] * 2 + [anywhere] * len(before),
        out_specs=anywhere,
        scratch_shapes=[pltpu.VMEM((width, cols), F32), pltpu.SemaphoreType.DMA((width // 128,))],
        input_output_aliases={2: 0} if before else {},
        compiler_params=pltpu.CompilerParams(vmem_limit_bytes=SMALL),
        name="sum_terms",
    )(mine, theirs, *before)


def act_kernel(where, weight_scale, codes, *refs):
    n = PIECES * len(WIDTHS)
    piece_refs, (away, keep, held, code_held, sem, code_sem) = refs[:n], refs[n:]
    code_copy = pltpu.make_async_copy(codes, code_held, code_sem)
    code_copy.start()
    rows = held.shape[1]
    for turn in Y_ORDER:
        lo = 0
        for i, width in enumerate(WIDTHS):
            window = pl.ds(lo, width)
            lo += width

            def load(ref, y, z):
                spot = pl.ds(pl.multiple_of(z * SHARD, SHARD), SHARD)
                pltpu.make_async_copy(ref, held.at[y, spot, window], sem.at[y]).start()

            each_shard(where, piece_refs[i * PIECES:(i + 1) * PIECES], load, (turn,))
    code_copy.wait()
    for turn in Y_ORDER:
        y = lax.rem(where[0] + turn + NY, NY)
        pltpu.make_async_copy(held.at[y], held.at[y], sem.at[y]).wait()
        total = jnp.dot(held[y], code_held[...], preferred_element_type=F32) * weight_scale[0]
        j = y ^ where[2]
        spot = pl.ds(pl.multiple_of((1 - j // 2) * rows, rows), rows)
        for out, side in ((away, 1), (keep, 0)):
            @pl.when(j % 2 == side)
            def _():
                out[spot, :] = total.astype(BF)


def act_parts(where, weight_scale, codes, groups):
    depth, cols = codes.shape
    rows = 8 * SHARD
    pieces = [piece for group in groups for piece in group]
    anywhere = pl.BlockSpec(memory_space=pltpu.HBM)
    smem = pl.BlockSpec(memory_space=pltpu.SMEM)
    return pl.pallas_call(
        act_kernel,
        out_shape=[jax.ShapeDtypeStruct((2 * rows, cols), BF)] * 2,
        in_specs=[smem, smem] + [anywhere] * (len(pieces) + 1),
        out_specs=[pl.BlockSpec(memory_space=pltpu.VMEM)] * 2,
        scratch_shapes=[
            pltpu.VMEM((4, rows, depth), BF),
            pltpu.VMEM((depth, cols), BF),
            pltpu.SemaphoreType.DMA((4,)),
            pltpu.SemaphoreType.DMA,
        ],
        compiler_params=pltpu.CompilerParams(vmem_limit_bytes=VMEM),
        cost_estimate=LITTLE,
        name="act_parts",
    )(where, weight_scale, codes, *pieces)


def finish_kernel(keep, got, other, rotated, bound, signs, out):
    rows = out.shape[0]
    summed = keep[rows:, :].astype(F32) + got[rows:, :].astype(F32) + other[...].astype(F32)
    masked = jnp.where(jnp.abs(rotated[...].astype(F32)) <= bound[...], summed, 0.0)
    high = masked.astype(BF)
    low = (masked - high.astype(F32)).astype(BF)
    table = signs[...]
    for lo in range(0, out.shape[1], HB):
        turned = jnp.dot(high[:, lo:lo + HB], table, preferred_element_type=F32)
        turned += jnp.dot(low[:, lo:lo + HB], table, preferred_element_type=F32)
        out[:, lo:lo + HB] = (turned * (HB ** -0.5)).astype(BF)


def finish(keep, got, other, rotated, bound, signs):
    vmem = pl.BlockSpec(memory_space=pltpu.VMEM)
    return pl.pallas_call(
        finish_kernel,
        out_shape=jax.ShapeDtypeStruct(other.shape, BF),
        in_specs=[vmem] * 6,
        out_specs=vmem,
        compiler_params=pltpu.CompilerParams(vmem_limit_bytes=SMALL),
        name="finish",
    )(keep, got, other, rotated, bound, signs)


def hadamard_signs(length):
    indices = jnp.arange(length, dtype=jnp.int32)
    common = indices[:, None] & indices[None, :]
    parity = jnp.zeros((length, length), jnp.int32)
    for bit in range(length.bit_length() - 1):
        parity = parity ^ (common >> bit)
    return (1 - 2 * (parity & 1)).astype(BF)


def body(cotangent, codes, weight_scale, rotated, clip_level):
    col = lax.axis_index("col")
    row = lax.axis_index("row")
    where = jnp.stack([col // NZ, col % NZ, row]).astype(jnp.int32)
    token_total = cotangent.shape[0] * lax.axis_size("col") * lax.axis_size("dp")
    grad_norm = token_total ** (-0.5)

    bound = clip_level[:, None]
    clipped = clip_turned(rotated, bound)
    tie = lax.optimization_barrier
    first_core = row % 2 == 0
    clips = [clipped, lax.ppermute(clipped, "row", CORE)]
    for pairs in (PARTNER, PARTNER_SIBLING):
        clips.append(lax.ppermute(clipped, ("dp", "row"), pairs))

    def before_second(*arrays):
        arrays = tie((*arrays, *clips[1:]))
        clips[1:] = arrays[-3:]
        return arrays[:-3]

    own = move(cotangent, (0, 0), (0, 0), True)
    groups = gather(own, first_core, before_second)
    mine0 = weight_term(where, groups[0], clips, grad_norm)
    theirs0 = lax.ppermute(mine0, "dp", DP)
    mine0, groups[0][0] = tie((mine0, groups[0][0]))
    rows = clipped.shape[1]
    away, keep = act_parts(where, weight_scale, codes, groups)
    away, keep, groups[1][0] = tie((away, keep, groups[1][0]))
    mine1 = weight_term(where, groups[1], clips, grad_norm)
    got = lax.ppermute(away, "row", CORE)
    outward = (keep[:rows].astype(F32) + got[:rows].astype(F32)).astype(BF)
    mine1, theirs0 = tie((mine1, theirs0))
    theirs1 = lax.ppermute(mine1, "dp", DP)
    inward = lax.ppermute(outward, ("dp", "row"), PARTNER)
    weight_grad = sum_terms(0, mine0, theirs0, None, codes.shape[0])
    input_grad = finish(keep, got, inward, rotated, bound, hadamard_signs(HB))
    input_grad, theirs1 = tie((input_grad, theirs1))
    weight_grad = sum_terms(WIDTHS[0], mine1, theirs1, weight_grad, codes.shape[0])
    return (input_grad, weight_grad)


def solution(mesh):
    placed = (
        P(("dp", "col"), "row"),
        P("row", "col"),
        P(),
        P(("dp", "row"), "col"),
        P(("dp", "row")),
    )
    return jax.shard_map(
        body,
        mesh=mesh,
        in_specs=placed,
        out_specs=(P(("dp", "row"), "col"), P("row", "col")),
        check_vma=False,
    )
```

```python
import functools

import jax
import jax.numpy as jnp
from jax import lax
from jax.experimental import pallas as pl
from jax.experimental.pallas import tpu as pltpu
from jax.sharding import PartitionSpec as P

HB = 128
NY, NZ = 4, 8
SHARD = 64
BF = jnp.bfloat16
F32 = jnp.float32

WIDTHS = (896, 896)
VMEM = 60 * 2**20
SMALL = 16 * 2**20
HALF = 512
LITTLE = pl.CostEstimate(flops=1, bytes_accessed=1, transcendentals=0)

NEAR = (-2, -1, 0, 1)
FAR = (-4, -3, 2, 3)
Y_ORDER = (0, -1, 1, -2)
PIECES = 10


def z_pairs(k):
    return [(y * NZ + z, y * NZ + (z + k) % NZ) for y in range(NY) for z in range(NZ)]


def y_pairs(k):
    return [(y * NZ + z, (y + k) % NY * NZ + z) for y in range(NY) for z in range(NZ)]


CORE = [(r, r ^ 1) for r in range(4)]
DP = [(0, 1), (1, 0)]
PARTNER_SIBLING = [(d * 4 + r, (1 - d) * 4 + (r ^ 3)) for d in range(2) for r in range(4)]
PARTNER = [(d * 4 + r, (1 - d) * 4 + (r ^ 2)) for d in range(2) for r in range(4)]


def pairs_for(steps, swap=False):
    pairs = []
    for d in range(2):
        for y in range(NY):
            for z in range(NZ):
                for r in range(4):
                    step = steps[r % 2]
                    if step is None:
                        continue
                    there = d ^ (y // 2 != r // 2) if swap else d
                    target = (y + step[0]) % NY * NZ + (z + step[1]) % NZ
                    pairs.append((((d * 32) + y * NZ + z) * 4 + r, (there * 32 + target) * 4 + r))
    return pairs


def move(value, core0, core1, swap=False):
    return lax.ppermute(value, ("dp", "col", "row"), pairs_for((core0, core1), swap))


def near_kernel(c, a, own, b, *outs):
    for i, shard in enumerate((c, a, own, b)):
        lo = 0
        for out in outs[:-2]:
            width = out.shape[1]
            out[i * SHARD:(i + 1) * SHARD, :] = shard[:, lo:lo + width]
            lo += width
        outs[-2 + i // 2][i % 2 * SHARD:(i % 2 + 1) * SHARD, :] = shard[...]


def far_kernel(low, high, *outs):
    lo = 0
    for out in outs:
        width = out.shape[1]
        out[:2 * SHARD, :] = low[:, lo:lo + width]
        out[2 * SHARD:, :] = high[:, lo:lo + width]
        lo += width


def join(kernel, shards, extra):
    vmem = pl.BlockSpec(memory_space=pltpu.VMEM)
    shapes = [(4 * SHARD, width) for width in WIDTHS] + extra
    return list(pl.pallas_call(
        kernel,
        out_shape=[jax.ShapeDtypeStruct(shape, BF) for shape in shapes],
        in_specs=[vmem] * len(shards),
        out_specs=[vmem] * len(shapes),
        compiler_params=pltpu.CompilerParams(vmem_limit_bytes=SMALL),
        cost_estimate=LITTLE,
        name="join",
    )(*shards))


def gather(own, first_core, before_second):
    a = move(own, (0, 1), (1, 0))
    b = move(own, (0, -1), (-1, 0))
    c = move(own, (0, 2), (2, 0))
    *near, low, high = join(near_kernel, (c, a, own, b), [(2 * SHARD, own.shape[1])] * 2)
    up1 = [move(near[0], (1, 0), (0, 1))]
    down1 = [move(near[0], (-1, 0), (0, -1))]
    low = move(low, (0, 2), None)
    high = move(high, (0, -2), None)
    near[1], low, high = before_second(near[1], low, high)
    up1.append(move(near[1], (1, 0), (0, 1)))
    down1.append(move(near[1], (-1, 0), (0, -1)))
    up2 = [move(part, (1, 0), (0, 1)) for part in up1]
    down2 = [move(part, None, (0, -1)) for part in down1]
    far = join(far_kernel, (low, high), [])
    up3 = [move(jnp.where(first_core, f, part), (1, 0), (0, 1)) for f, part in zip(far, up2)]
    down3 = [move(jnp.where(first_core, f, part), (-1, 0), (0, -1)) for f, part in zip(far, down2)]
    up4 = [move(part[:2 * SHARD], (1, 0), (0, 1)) for part in up3]
    down4 = [move(part[2 * SHARD:], (-1, 0), (0, -1)) for part in down3]
    return [list(group) for group in zip(near, far, up1, down1, up2, down2, up3, down3, up4, down4)]


def places_of(core):
    if core == 0:
        lines = ((0, NEAR), (0, FAR), (-1, NEAR), (1, NEAR), (-2, NEAR), (0, ()), (-1, FAR), (1, FAR),
                 (-2, FAR[:2]), (-2, FAR[2:]))
        return [[(dy, dz) for dz in line] for dy, line in lines]
    lines = ((0, NEAR), (0, ()), (-1, NEAR), (1, NEAR), (-2, NEAR), (2, NEAR), (-3, NEAR), (3, NEAR),
             (-4, NEAR[:2]), (4, NEAR[2:]))
    return [[(dy, dz) for dy in line] for dz, line in lines]


def each_shard(where, refs, do, turns=Y_ORDER):
    for core in range(2):
        @pl.when(where[2] % 2 == core)
        def _():
            for turn in turns:
                for ref, spots in zip(refs, places_of(core)):
                    for at, (dy, dz) in enumerate(spots):
                        if dy == turn:
                            do(ref.at[pl.ds(at * SHARD, SHARD)],
                               lax.rem(where[0] + dy + NY, NY), lax.rem(where[1] + dz + NZ, NZ))


def clip_kernel(rotated, bound, out):
    top = bound[...]
    for lo in range(0, rotated.shape[1], 128):
        block = jnp.clip(rotated[:, lo:lo + 128].astype(F32), -top, top)
        out[lo:lo + 128, :] = block.T.astype(BF)


def clip_turned(rotated, bound):
    vmem = pl.BlockSpec(memory_space=pltpu.VMEM)
    return pl.pallas_call(
        clip_kernel,
        out_shape=jax.ShapeDtypeStruct(rotated.shape[::-1], BF),
        in_specs=[vmem] * 2,
        out_specs=vmem,
        compiler_params=pltpu.CompilerParams(vmem_limit_bytes=SMALL),
        name="clip_turned",
    )(rotated, bound)


def weight_kernel(scale, where, *refs):
    n = PIECES
    piece_refs, clip_refs = refs[:n], refs[n:n + 4]
    out, held, clip_held, sem, clip_sem = refs[n + 4:]
    for j, ref in enumerate(clip_refs):
        size = ref.shape[1]
        start = pl.multiple_of((where[2] ^ j) * size, size)
        pltpu.make_async_copy(ref, clip_held.at[:, pl.ds(start, size)], clip_sem).start()
    width = out.shape[1]
    windows = ((0, HALF), (HALF, width))
    for i, (lo, hi) in enumerate(windows):
        window = pl.ds(lo, hi - lo)

        def load(ref, y, z):
            spot = pl.ds(pl.multiple_of((y * NZ + z) * SHARD, SHARD), SHARD)
            pltpu.make_async_copy(ref.at[:, window], held.at[spot, window], sem.at[i]).start()

        each_shard(where, piece_refs, load)
    pltpu.make_async_copy(clip_held, clip_held, clip_sem).wait()
    for i, (lo, hi) in enumerate(windows):
        part = held.at[:, pl.ds(lo, hi - lo)]
        pltpu.make_async_copy(part, part, sem.at[i]).wait()
        for first in range(lo, hi, 256):
            step = min(256, hi - first)
            out[:, first:first + step] = (
                jnp.dot(clip_held[...], held[:, first:first + step], preferred_element_type=F32) * scale
            ).astype(BF)


def weight_term(where, pieces, clips, scale):
    width = pieces[0].shape[1]
    cols, part = clips[0].shape
    tokens = 4 * part
    anywhere = pl.BlockSpec(memory_space=pltpu.HBM)
    return pl.pallas_call(
        functools.partial(weight_kernel, scale),
        out_shape=jax.ShapeDtypeStruct((cols, width), BF),
        in_specs=[pl.BlockSpec(memory_space=pltpu.SMEM)] + [anywhere] * (len(pieces) + 4),
        out_specs=pl.BlockSpec(memory_space=pltpu.VMEM),
        scratch_shapes=[
            pltpu.VMEM((tokens, width), BF),
            pltpu.VMEM((cols, tokens), BF),
            pltpu.SemaphoreType.DMA((2,)),
            pltpu.SemaphoreType.DMA,
        ],
        compiler_params=pltpu.CompilerParams(vmem_limit_bytes=VMEM),
        cost_estimate=pl.CostEstimate(
            flops=2 * tokens * width * cols,
            bytes_accessed=2 * (tokens * (width + cols) + width * cols),
            transcendentals=0),
        name="weight_term",
    )(where, *pieces, *clips)


def sum_kernel(lo, mine, theirs, *refs):
    out, held, sem = refs[-3:]
    width = mine.shape[1]
    copies = []
    for at in range(0, width, 128):
        both = mine[:, at:at + 128].astype(F32) + theirs[:, at:at + 128].astype(F32)
        held[at:at + 128, :] = both.T
        copies.append(pltpu.make_async_copy(
            held.at[pl.ds(at, 128)], out.at[pl.ds(lo + at, 128)], sem.at[at // 128]))
        copies[-1].start()
    for copy in copies:
        copy.wait()


def sum_terms(lo, mine, theirs, whole, depth):
    cols, width = mine.shape
    vmem = pl.BlockSpec(memory_space=pltpu.VMEM)
    anywhere = pl.BlockSpec(memory_space=pltpu.HBM)
    before = [] if whole is None else [whole]
    return pl.pallas_call(
        functools.partial(sum_kernel, lo),
        out_shape=jax.ShapeDtypeStruct((depth, cols), F32),
        in_specs=[vmem] * 2 + [anywhere] * len(before),
        out_specs=anywhere,
        scratch_shapes=[pltpu.VMEM((width, cols), F32), pltpu.SemaphoreType.DMA((width // 128,))],
        input_output_aliases={2: 0} if before else {},
        compiler_params=pltpu.CompilerParams(vmem_limit_bytes=SMALL),
        name="sum_terms",
    )(mine, theirs, *before)


def act_kernel(where, weight_scale, codes, *refs):
    n = PIECES * len(WIDTHS)
    piece_refs, (away, keep, held, code_held, sem, code_sem) = refs[:n], refs[n:]
    code_copy = pltpu.make_async_copy(codes, code_held, code_sem)
    code_copy.start()
    rows = held.shape[1]
    for turn in Y_ORDER:
        lo = 0
        for i, width in enumerate(WIDTHS):
            window = pl.ds(lo, width)
            lo += width

            def load(ref, y, z):
                spot = pl.ds(pl.multiple_of(z * SHARD, SHARD), SHARD)
                pltpu.make_async_copy(ref, held.at[y, spot, window], sem.at[y]).start()

            each_shard(where, piece_refs[i * PIECES:(i + 1) * PIECES], load, (turn,))
    code_copy.wait()
    for turn in Y_ORDER:
        y = lax.rem(where[0] + turn + NY, NY)
        pltpu.make_async_copy(held.at[y], held.at[y], sem.at[y]).wait()
        total = jnp.dot(held[y], code_held[...], preferred_element_type=F32) * weight_scale[0]
        j = y ^ where[2]
        spot = pl.ds(pl.multiple_of((1 - j // 2) * rows, rows), rows)
        for out, side in ((away, 1), (keep, 0)):
            @pl.when(j % 2 == side)
            def _():
                out[spot, :] = total.astype(BF)


def act_parts(where, weight_scale, codes, groups):
    depth, cols = codes.shape
    rows = 8 * SHARD
    pieces = [piece for group in groups for piece in group]
    anywhere = pl.BlockSpec(memory_space=pltpu.HBM)
    smem = pl.BlockSpec(memory_space=pltpu.SMEM)
    return pl.pallas_call(
        act_kernel,
        out_shape=[jax.ShapeDtypeStruct((2 * rows, cols), BF)] * 2,
        in_specs=[smem, smem] + [anywhere] * (len(pieces) + 1),
        out_specs=[pl.BlockSpec(memory_space=pltpu.VMEM)] * 2,
        scratch_shapes=[
            pltpu.VMEM((4, rows, depth), BF),
            pltpu.VMEM((depth, cols), BF),
            pltpu.SemaphoreType.DMA((4,)),
            pltpu.SemaphoreType.DMA,
        ],
        compiler_params=pltpu.CompilerParams(vmem_limit_bytes=VMEM),
        cost_estimate=LITTLE,
        name="act_parts",
    )(where, weight_scale, codes, *pieces)


def finish_kernel(keep, got, other, rotated, bound, signs, out):
    rows = out.shape[0]
    summed = keep[rows:, :].astype(F32) + got[rows:, :].astype(F32) + other[...].astype(F32)
    masked = jnp.where(jnp.abs(rotated[...].astype(F32)) <= bound[...], summed, 0.0)
    high = masked.astype(BF)
    low = (masked - high.astype(F32)).astype(BF)
    table = signs[...]
    for lo in range(0, out.shape[1], HB):
        turned = jnp.dot(high[:, lo:lo + HB], table, preferred_element_type=F32)
        turned += jnp.dot(low[:, lo:lo + HB], table, preferred_element_type=F32)
        out[:, lo:lo + HB] = (turned * (HB ** -0.5)).astype(BF)


def finish(keep, got, other, rotated, bound, signs):
    vmem = pl.BlockSpec(memory_space=pltpu.VMEM)
    return pl.pallas_call(
        finish_kernel,
        out_shape=jax.ShapeDtypeStruct(other.shape, BF),
        in_specs=[vmem] * 6,
        out_specs=vmem,
        compiler_params=pltpu.CompilerParams(vmem_limit_bytes=SMALL),
        name="finish",
    )(keep, got, other, rotated, bound, signs)


def hadamard_signs(length):
    indices = jnp.arange(length, dtype=jnp.int32)
    common = indices[:, None] & indices[None, :]
    parity = jnp.zeros((length, length), jnp.int32)
    for bit in range(length.bit_length() - 1):
        parity = parity ^ (common >> bit)
    return (1 - 2 * (parity & 1)).astype(BF)


def body(cotangent, codes, weight_scale, rotated, clip_level):
    col = lax.axis_index("col")
    row = lax.axis_index("row")
    where = jnp.stack([col // NZ, col % NZ, row]).astype(jnp.int32)
    token_total = cotangent.shape[0] * lax.axis_size("col") * lax.axis_size("dp")
    grad_norm = token_total ** (-0.5)

    bound = clip_level[:, None]
    clipped = clip_turned(rotated, bound)
    tie = lax.optimization_barrier
    first_core = row % 2 == 0
    clips = [clipped, lax.ppermute(clipped, "row", CORE)]
    for pairs in (PARTNER, PARTNER_SIBLING):
        clips.append(lax.ppermute(clipped, ("dp", "row"), pairs))

    def before_second(*arrays):
        arrays = tie((*arrays, *clips[1:]))
        clips[1:] = arrays[-3:]
        return arrays[:-3]

    own = move(cotangent, (0, 0), (0, 0), True)
    own, where = tie((own, where))
    groups = gather(own, first_core, before_second)
    mine0 = weight_term(where, groups[0], clips, grad_norm)
    theirs0 = lax.ppermute(mine0, "dp", DP)
    mine0, groups[0][0] = tie((mine0, groups[0][0]))
    rows = clipped.shape[1]
    away, keep = act_parts(where, weight_scale, codes, groups)
    away, keep, groups[1][0] = tie((away, keep, groups[1][0]))
    mine1 = weight_term(where, groups[1], clips, grad_norm)
    got = lax.ppermute(away, "row", CORE)
    outward = (keep[:rows].astype(F32) + got[:rows].astype(F32)).astype(BF)
    mine1, theirs0 = tie((mine1, theirs0))
    theirs1 = lax.ppermute(mine1, "dp", DP)
    inward = lax.ppermute(outward, ("dp", "row"), PARTNER)
    weight_grad = sum_terms(0, mine0, theirs0, None, codes.shape[0])
    input_grad = finish(keep, got, inward, rotated, bound, hadamard_signs(HB))
    input_grad, theirs1 = tie((input_grad, theirs1))
    weight_grad = sum_terms(WIDTHS[0], mine1, theirs1, weight_grad, codes.shape[0])
    return (input_grad, weight_grad)


def solution(mesh):
    placed = (
        P(("dp", "col"), "row"),
        P("row", "col"),
        P(),
        P(("dp", "row"), "col"),
        P(("dp", "row")),
    )
    return jax.shard_map(
        body,
        mesh=mesh,
        in_specs=placed,
        out_specs=(P(("dp", "row"), "col"), P("row", "col")),
        check_vma=False,
    )
```

```python
import functools

import jax
import jax.numpy as jnp
from jax import lax
from jax.experimental import pallas as pl
from jax.experimental.pallas import tpu as pltpu
from jax.sharding import PartitionSpec as P

HB = 128
NY, NZ = 4, 8
SHARD = 64
BF = jnp.bfloat16
F32 = jnp.float32

WIDTHS = (896, 896)
VMEM = 60 * 2**20
SMALL = 16 * 2**20
HALF = 256
LITTLE = pl.CostEstimate(flops=1, bytes_accessed=1, transcendentals=0)

NEAR = (-2, -1, 0, 1)
FAR = (-4, -3, 2, 3)
Y_ORDER = (0, -1, 1, -2)
PIECES = 10


def z_pairs(k):
    return [(y * NZ + z, y * NZ + (z + k) % NZ) for y in range(NY) for z in range(NZ)]


def y_pairs(k):
    return [(y * NZ + z, (y + k) % NY * NZ + z) for y in range(NY) for z in range(NZ)]


CORE = [(r, r ^ 1) for r in range(4)]
DP = [(0, 1), (1, 0)]
PARTNER_SIBLING = [(d * 4 + r, (1 - d) * 4 + (r ^ 3)) for d in range(2) for r in range(4)]
PARTNER = [(d * 4 + r, (1 - d) * 4 + (r ^ 2)) for d in range(2) for r in range(4)]


def pairs_for(steps, swap=False):
    pairs = []
    for d in range(2):
        for y in range(NY):
            for z in range(NZ):
                for r in range(4):
                    step = steps[r % 2]
                    if step is None:
                        continue
                    there = d ^ (y // 2 != r // 2) if swap else d
                    target = (y + step[0]) % NY * NZ + (z + step[1]) % NZ
                    pairs.append((((d * 32) + y * NZ + z) * 4 + r, (there * 32 + target) * 4 + r))
    return pairs


def move(value, core0, core1, swap=False):
    return lax.ppermute(value, ("dp", "col", "row"), pairs_for((core0, core1), swap))


def near_kernel(c, a, own, b, *outs):
    for i, shard in enumerate((c, a, own, b)):
        lo = 0
        for out in outs[:-2]:
            width = out.shape[1]
            out[i * SHARD:(i + 1) * SHARD, :] = shard[:, lo:lo + width]
            lo += width
        outs[-2 + i // 2][i % 2 * SHARD:(i % 2 + 1) * SHARD, :] = shard[...]


def far_kernel(low, high, *outs):
    lo = 0
    for out in outs:
        width = out.shape[1]
        out[:2 * SHARD, :] = low[:, lo:lo + width]
        out[2 * SHARD:, :] = high[:, lo:lo + width]
        lo += width


def join(kernel, shards, extra):
    vmem = pl.BlockSpec(memory_space=pltpu.VMEM)
    shapes = [(4 * SHARD, width) for width in WIDTHS] + extra
    return list(pl.pallas_call(
        kernel,
        out_shape=[jax.ShapeDtypeStruct(shape, BF) for shape in shapes],
        in_specs=[vmem] * len(shards),
        out_specs=[vmem] * len(shapes),
        compiler_params=pltpu.CompilerParams(vmem_limit_bytes=SMALL),
        cost_estimate=LITTLE,
        name="join",
    )(*shards))


def gather(own, first_core, before_second):
    a = move(own, (0, 1), (1, 0))
    b = move(own, (0, -1), (-1, 0))
    c = move(own, (0, 2), (2, 0))
    *near, low, high = join(near_kernel, (c, a, own, b), [(2 * SHARD, own.shape[1])] * 2)
    up1 = [move(near[0], (1, 0), (0, 1))]
    down1 = [move(near[0], (-1, 0), (0, -1))]
    low = move(low, (0, 2), None)
    high = move(high, (0, -2), None)
    near[1], low, high = before_second(near[1], low, high)
    up1.append(move(near[1], (1, 0), (0, 1)))
    down1.append(move(near[1], (-1, 0), (0, -1)))
    up2 = [move(part, (1, 0), (0, 1)) for part in up1]
    down2 = [move(part, None, (0, -1)) for part in down1]
    far = join(far_kernel, (low, high), [])
    up3 = [move(jnp.where(first_core, f, part), (1, 0), (0, 1)) for f, part in zip(far, up2)]
    down3 = [move(jnp.where(first_core, f, part), (-1, 0), (0, -1)) for f, part in zip(far, down2)]
    up4 = [move(part[:2 * SHARD], (1, 0), (0, 1)) for part in up3]
    down4 = [move(part[2 * SHARD:], (-1, 0), (0, -1)) for part in down3]
    return [list(group) for group in zip(near, far, up1, down1, up2, down2, up3, down3, up4, down4)]


def places_of(core):
    if core == 0:
        lines = ((0, NEAR), (0, FAR), (-1, NEAR), (1, NEAR), (-2, NEAR), (0, ()), (-1, FAR), (1, FAR),
                 (-2, FAR[:2]), (-2, FAR[2:]))
        return [[(dy, dz) for dz in line] for dy, line in lines]
    lines = ((0, NEAR), (0, ()), (-1, NEAR), (1, NEAR), (-2, NEAR), (2, NEAR), (-3, NEAR), (3, NEAR),
             (-4, NEAR[:2]), (4, NEAR[2:]))
    return [[(dy, dz) for dy in line] for dz, line in lines]


def each_shard(where, refs, do, turns=Y_ORDER):
    for core in range(2):
        @pl.when(where[2] % 2 == core)
        def _():
            for turn in turns:
                for ref, spots in zip(refs, places_of(core)):
                    for at, (dy, dz) in enumerate(spots):
                        if dy == turn:
                            do(ref.at[pl.ds(at * SHARD, SHARD)],
                               lax.rem(where[0] + dy + NY, NY), lax.rem(where[1] + dz + NZ, NZ))


def clip_kernel(rotated, bound, out):
    top = bound[...]
    for lo in range(0, rotated.shape[1], 128):
        block = jnp.clip(rotated[:, lo:lo + 128].astype(F32), -top, top)
        out[lo:lo + 128, :] = block.T.astype(BF)


def clip_turned(rotated, bound):
    vmem = pl.BlockSpec(memory_space=pltpu.VMEM)
    return pl.pallas_call(
        clip_kernel,
        out_shape=jax.ShapeDtypeStruct(rotated.shape[::-1], BF),
        in_specs=[vmem] * 2,
        out_specs=vmem,
        compiler_params=pltpu.CompilerParams(vmem_limit_bytes=SMALL),
        name="clip_turned",
    )(rotated, bound)


def weight_kernel(scale, where, *refs):
    n = PIECES
    piece_refs, clip_refs = refs[:n], refs[n:n + 4]
    out, made, held, clip_held, sem, clip_sem, out_sem = refs[n + 4:]
    for j, ref in enumerate(clip_refs):
        size = ref.shape[1]
        start = pl.multiple_of((where[2] ^ j) * size, size)
        pltpu.make_async_copy(ref, clip_held.at[:, pl.ds(start, size)], clip_sem).start()
    width = out.shape[1]
    windows = ((0, HALF), (HALF, width))
    for i, (lo, hi) in enumerate(windows):
        window = pl.ds(lo, hi - lo)

        def load(ref, y, z):
            spot = pl.ds(pl.multiple_of((y * NZ + z) * SHARD, SHARD), SHARD)
            pltpu.make_async_copy(ref.at[:, window], held.at[spot, window], sem.at[i]).start()

        each_shard(where, piece_refs, load)
    outward = []
    pltpu.make_async_copy(clip_held, clip_held, clip_sem).wait()
    for i, (lo, hi) in enumerate(windows):
        part = held.at[:, pl.ds(lo, hi - lo)]
        pltpu.make_async_copy(part, part, sem.at[i]).wait()
        for first in range(lo, hi, 256):
            step = min(256, hi - first)
            made[:, first:first + step] = (
                jnp.dot(clip_held[...], held[:, first:first + step], preferred_element_type=F32) * scale
            ).astype(BF)
            tile = pl.ds(first, step)
            outward.append(pltpu.make_async_copy(made.at[:, tile], out.at[:, tile], out_sem.at[len(outward)]))
            outward[-1].start()
    for copy in outward:
        copy.wait()


def weight_term(where, pieces, clips, scale):
    width = pieces[0].shape[1]
    cols, part = clips[0].shape
    tokens = 4 * part
    anywhere = pl.BlockSpec(memory_space=pltpu.HBM)
    return pl.pallas_call(
        functools.partial(weight_kernel, scale),
        out_shape=jax.ShapeDtypeStruct((cols, width), BF),
        in_specs=[pl.BlockSpec(memory_space=pltpu.SMEM)] + [anywhere] * (len(pieces) + 4),
        out_specs=anywhere,
        scratch_shapes=[
            pltpu.VMEM((cols, width), BF),
            pltpu.VMEM((tokens, width), BF),
            pltpu.VMEM((cols, tokens), BF),
            pltpu.SemaphoreType.DMA((2,)),
            pltpu.SemaphoreType.DMA,
            pltpu.SemaphoreType.DMA((width // 128,)),
        ],
        compiler_params=pltpu.CompilerParams(vmem_limit_bytes=VMEM),
        cost_estimate=pl.CostEstimate(
            flops=2 * tokens * width * cols,
            bytes_accessed=2 * (tokens * (width + cols) + width * cols),
            transcendentals=0),
        name="weight_term",
    )(where, *pieces, *clips)


def sum_kernel(lo, mine, theirs, *refs):
    out, held, sem = refs[-3:]
    width = mine.shape[1]
    copies = []
    for at in range(0, width, 128):
        both = mine[:, at:at + 128].astype(F32) + theirs[:, at:at + 128].astype(F32)
        held[at:at + 128, :] = both.T
        copies.append(pltpu.make_async_copy(
            held.at[pl.ds(at, 128)], out.at[pl.ds(lo + at, 128)], sem.at[at // 128]))
        copies[-1].start()
    for copy in copies:
        copy.wait()


def sum_terms(lo, mine, theirs, whole, depth):
    cols, width = mine.shape
    vmem = pl.BlockSpec(memory_space=pltpu.VMEM)
    anywhere = pl.BlockSpec(memory_space=pltpu.HBM)
    before = [] if whole is None else [whole]
    return pl.pallas_call(
        functools.partial(sum_kernel, lo),
        out_shape=jax.ShapeDtypeStruct((depth, cols), F32),
        in_specs=[vmem] * 2 + [anywhere] * len(before),
        out_specs=anywhere,
        scratch_shapes=[pltpu.VMEM((width, cols), F32), pltpu.SemaphoreType.DMA((width // 128,))],
        input_output_aliases={2: 0} if before else {},
        compiler_params=pltpu.CompilerParams(vmem_limit_bytes=SMALL),
        name="sum_terms",
    )(mine, theirs, *before)


def act_kernel(where, weight_scale, codes, *refs):
    n = PIECES * len(WIDTHS)
    piece_refs, (away, keep, held, code_held, sem, code_sem) = refs[:n], refs[n:]
    code_copy = pltpu.make_async_copy(codes, code_held, code_sem)
    code_copy.start()
    rows = held.shape[1]
    for turn in Y_ORDER:
        lo = 0
        for i, width in enumerate(WIDTHS):
            window = pl.ds(lo, width)
            lo += width

            def load(ref, y, z):
                spot = pl.ds(pl.multiple_of(z * SHARD, SHARD), SHARD)
                pltpu.make_async_copy(ref, held.at[y, spot, window], sem.at[y]).start()

            each_shard(where, piece_refs[i * PIECES:(i + 1) * PIECES], load, (turn,))
    code_copy.wait()
    for turn in Y_ORDER:
        y = lax.rem(where[0] + turn + NY, NY)
        pltpu.make_async_copy(held.at[y], held.at[y], sem.at[y]).wait()
        total = jnp.dot(held[y], code_held[...], preferred_element_type=F32) * weight_scale[0]
        j = y ^ where[2]
        spot = pl.ds(pl.multiple_of((1 - j // 2) * rows, rows), rows)
        for out, side in ((away, 1), (keep, 0)):
            @pl.when(j % 2 == side)
            def _():
                out[spot, :] = total.astype(BF)


def act_parts(where, weight_scale, codes, groups):
    depth, cols = codes.shape
    rows = 8 * SHARD
    pieces = [piece for group in groups for piece in group]
    anywhere = pl.BlockSpec(memory_space=pltpu.HBM)
    smem = pl.BlockSpec(memory_space=pltpu.SMEM)
    return pl.pallas_call(
        act_kernel,
        out_shape=[jax.ShapeDtypeStruct((2 * rows, cols), BF)] * 2,
        in_specs=[smem, smem] + [anywhere] * (len(pieces) + 1),
        out_specs=[pl.BlockSpec(memory_space=pltpu.VMEM)] * 2,
        scratch_shapes=[
            pltpu.VMEM((4, rows, depth), BF),
            pltpu.VMEM((depth, cols), BF),
            pltpu.SemaphoreType.DMA((4,)),
            pltpu.SemaphoreType.DMA,
        ],
        compiler_params=pltpu.CompilerParams(vmem_limit_bytes=VMEM),
        cost_estimate=LITTLE,
        name="act_parts",
    )(where, weight_scale, codes, *pieces)


def finish_kernel(keep, got, other, rotated, bound, signs, out):
    rows = out.shape[0]
    summed = keep[rows:, :].astype(F32) + got[rows:, :].astype(F32) + other[...].astype(F32)
    masked = jnp.where(jnp.abs(rotated[...].astype(F32)) <= bound[...], summed, 0.0)
    high = masked.astype(BF)
    low = (masked - high.astype(F32)).astype(BF)
    table = signs[...]
    for lo in range(0, out.shape[1], HB):
        turned = jnp.dot(high[:, lo:lo + HB], table, preferred_element_type=F32)
        turned += jnp.dot(low[:, lo:lo + HB], table, preferred_element_type=F32)
        out[:, lo:lo + HB] = (turned * (HB ** -0.5)).astype(BF)


def finish(keep, got, other, rotated, bound, signs):
    vmem = pl.BlockSpec(memory_space=pltpu.VMEM)
    return pl.pallas_call(
        finish_kernel,
        out_shape=jax.ShapeDtypeStruct(other.shape, BF),
        in_specs=[vmem] * 6,
        out_specs=vmem,
        compiler_params=pltpu.CompilerParams(vmem_limit_bytes=SMALL),
        name="finish",
    )(keep, got, other, rotated, bound, signs)


def hadamard_signs(length):
    indices = jnp.arange(length, dtype=jnp.int32)
    common = indices[:, None] & indices[None, :]
    parity = jnp.zeros((length, length), jnp.int32)
    for bit in range(length.bit_length() - 1):
        parity = parity ^ (common >> bit)
    return (1 - 2 * (parity & 1)).astype(BF)


def body(cotangent, codes, weight_scale, rotated, clip_level):
    col = lax.axis_index("col")
    row = lax.axis_index("row")
    where = jnp.stack([col // NZ, col % NZ, row]).astype(jnp.int32)
    token_total = cotangent.shape[0] * lax.axis_size("col") * lax.axis_size("dp")
    grad_norm = token_total ** (-0.5)

    bound = clip_level[:, None]
    clipped = clip_turned(rotated, bound)
    tie = lax.optimization_barrier
    first_core = row % 2 == 0
    clips = [clipped, lax.ppermute(clipped, "row", CORE)]
    for pairs in (PARTNER, PARTNER_SIBLING):
        clips.append(lax.ppermute(clipped, ("dp", "row"), pairs))

    def before_second(*arrays):
        arrays = tie((*arrays, *clips[1:]))
        clips[1:] = arrays[-3:]
        return arrays[:-3]

    own = move(cotangent, (0, 0), (0, 0), True)
    own, where = tie((own, where))
    groups = gather(own, first_core, before_second)
    mine0 = weight_term(where, groups[0], clips, grad_norm)
    theirs0 = lax.ppermute(mine0, "dp", DP)
    mine0, groups[0][0] = tie((mine0, groups[0][0]))
    rows = clipped.shape[1]
    away, keep = act_parts(where, weight_scale, codes, groups)
    away, keep, groups[1][0] = tie((away, keep, groups[1][0]))
    mine1 = weight_term(where, groups[1], clips, grad_norm)
    got = lax.ppermute(away, "row", CORE)
    outward = (keep[:rows].astype(F32) + got[:rows].astype(F32)).astype(BF)
    mine1, theirs0 = tie((mine1, theirs0))
    theirs1 = lax.ppermute(mine1, "dp", DP)
    inward = lax.ppermute(outward, ("dp", "row"), PARTNER)
    weight_grad = sum_terms(0, mine0, theirs0, None, codes.shape[0])
    input_grad = finish(keep, got, inward, rotated, bound, hadamard_signs(HB))
    input_grad, theirs1 = tie((input_grad, theirs1))
    weight_grad = sum_terms(WIDTHS[0], mine1, theirs1, weight_grad, codes.shape[0])
    return (input_grad, weight_grad)


def solution(mesh):
    placed = (
        P(("dp", "col"), "row"),
        P("row", "col"),
        P(),
        P(("dp", "row"), "col"),
        P(("dp", "row")),
    )
    return jax.shard_map(
        body,
        mesh=mesh,
        in_specs=placed,
        out_specs=(P(("dp", "row"), "col"), P("row", "col")),
        check_vma=False,
    )
```
